32 devices in a mesh: tm: 4 (over y, core), sta: 8 (over z, x).
Axes of the slice: x: 2, y: 2, z: 4, core: 2. Of those that a mesh axis runs over, the one named last changes fastest.
Arguments:
- spectra: bfloat16 [4, 512, 2048], P('tm', 'sta'), may hold values from -5 to 5
- pair_list: int32 [4, 8, 256], P('tm', 'sta'), may hold values from 0 to 511, as said below
- pair_stations: int32 [2, 4096], P(None, 'sta'), may hold values from 0 to 511
- owner_code: int32 [4096], P('sta'), may hold values from 0 to 1023, as said below
Outputs:
- stack: float32 [8192, 1024], P(('tm', 'sta'))
The draws below stay inside these ranges and needn't reach their ends.
Inputs may be any that keep to these rules, and one draw needn't show every extreme that they name: `pair_list`: within each (g, s) the entries are distinct catalogue numbers below 512. `owner_code`: within each catalogue of 512 pairs the codes are distinct; each owner (code // 256) holds at most 256 pairs of a catalogue, and in every catalogue one owner holds exactly 256.
All inputs are finite; a program needn't handle non-finite values.
Results may differ from the reference program's by a relative error of at most 0.0003.
Values may be sent and summed in bfloat16 or wider, within the bound.
No kernel may reach another device: no remote copies, remote signals or barrier semaphores. Data moves between devices by JAX's collectives and lax.ppermute only.
A program may use at most 64 MiB of HBM per device.

```python
import jax
import jax.numpy as jnp
from jax import lax

FREQUENCY_BINS = 1024
LAGS = 1024
P_DEV = 256
PCOL = 512
NPAIR = 4096
S = 512
CAP = 256
STACK_SLOT_COUNT = 8192
N_TM = 4
N_STA = 8


def draw_pair_list(key, part):
    keys = jax.random.split(key, N_TM * N_STA)
    picked = jax.vmap(lambda single: jax.random.permutation(single, PCOL)[:P_DEV])(keys)
    return picked.reshape(N_TM, N_STA, P_DEV).astype(jnp.int32)


def draw_owner_code(key, part):
    keys = jax.random.split(jax.random.fold_in(key, 7), N_STA)

    def single_column(single):
        first_key, second_key, tertiary_key = jax.random.split(single, 3)
        complete_owner = jax.random.randint(first_key, (), 0, N_TM)
        codes_all = jnp.arange(N_TM * CAP, dtype=jnp.int32)
        ranking = jax.random.permutation(second_key, N_TM * CAP).astype(jnp.int32)
        forced = (codes_all // CAP == complete_owner) | (codes_all == 0) | (codes_all == N_TM * CAP - 1)
        score = jnp.where(forced, 0, 1 + ranking)
        chosen = codes_all[jnp.argsort(score, stable=True)][:PCOL]
        return jax.random.permutation(tertiary_key, chosen)
    return jax.vmap(single_column)(keys).reshape(-1).astype(jnp.int32)


def with_ends(entries, own_key, smallest, largest):
    shape = entries.shape
    spot = [jax.random.randint(jax.random.fold_in(own_key, axis), (), 0, shape[axis]) for axis in range(len(shape))]
    entries = entries.at[tuple(spot)].set(smallest)
    longest = shape.index(max(shape))
    spot[longest] = (spot[longest] + 1) % shape[longest]
    return entries.at[tuple(spot)].set(largest)


def shard_levels(own_key, extent, cuts, smallest, high):
    factor_of = 1.0
    for axis_at, shards_of in cuts:
        draws = jax.random.uniform(jax.random.fold_in(jax.random.fold_in(own_key, 6), axis_at), (shards_of,), jnp.float32, smallest / len(cuts), high / len(cuts))
        factor_of = factor_of * jnp.repeat(jnp.exp(draws), extent[axis_at] // shards_of).reshape((-1,) + (1,) * (len(extent) - 1 - axis_at))
    return factor_of


def gaussian(own_key, shape, deviation, limit, shards=(), kind=jnp.bfloat16):
    entries = deviation * jax.random.normal(own_key, shape, jnp.float32)
    if shards:
        entries = entries * shard_levels(own_key, shape, shards, -0.22, 0.18)
    return jnp.clip(entries, -limit, limit).astype(kind)


def setup_inputs(seed: int = 0) -> dict:
    seeds = jax.random.split(jax.random.key(seed), 5)
    return {
        "spectra": gaussian(seeds[0], (N_TM, S, 2 * FREQUENCY_BINS), 0.7, 5.0, ((0, 4), (1, 8))),
        "pair_list": draw_pair_list(jax.random.fold_in(seeds[4], 71), 0),
        "pair_stations": with_ends(jax.random.randint(seeds[2], (2, NPAIR), 0, S), jax.random.fold_in(seeds[2], 1), 0, S - 1).astype(jnp.int32),
        "owner_code": draw_owner_code(jax.random.fold_in(seeds[4], 71), 0),
    }


def lag_table(bins, lags):
    bin_index = jnp.arange(bins, dtype=jnp.int32)[:, None]
    lag_index = jnp.arange(lags, dtype=jnp.int32)[None, :] - lags // 2
    phase = ((bin_index * lag_index) % (2 * bins)).astype(jnp.float32) * (jnp.pi / bins)
    scale = 1.0 / (bins ** 0.5)
    return jnp.concatenate([jnp.cos(phase) * scale, -jnp.sin(phase) * scale], axis=0)


def cross_spectra(first, second, bins):
    first = first.astype(jnp.float32)
    second = second.astype(jnp.float32)
    real_a, imag_a = first[..., :bins], first[..., bins:]
    real_b, imag_b = second[..., :bins], second[..., bins:]
    real_c = real_a * real_b + imag_a * imag_b
    imag_c = real_a * imag_b - imag_a * real_b
    return jnp.concatenate([real_c, imag_c], axis=-1)


def reference(spectra, pair_list, pair_stations, owner_code):
    column_entry = jnp.arange(N_STA, dtype=jnp.int32)[:, None]

    def single_group(group, running_totals):
        listed = pair_list[group] + column_entry * PCOL
        first = spectra[group][pair_stations[0][listed]]
        second = spectra[group][pair_stations[1][listed]]
        cross = cross_spectra(first, second, FREQUENCY_BINS)
        codes = owner_code[listed]
        rows = (codes // CAP) * (N_STA * CAP) + column_entry * CAP + codes % CAP
        return running_totals.at[rows.reshape(-1)].add(cross.reshape(-1, 2 * FREQUENCY_BINS))

    running_totals = lax.fori_loop(0, N_TM, single_group, jnp.zeros((STACK_SLOT_COUNT, 2 * FREQUENCY_BINS), jnp.float32))
    return jnp.dot(running_totals, lag_table(FREQUENCY_BINS, LAGS), precision=lax.Precision.HIGHEST, preferred_element_type=jnp.float32)
```

```python
import functools

import jax
import jax.numpy as jnp
import numpy as np
from jax import lax
from jax.experimental import pallas as pl
from jax.experimental.pallas import tpu as pltpu
from jax.sharding import PartitionSpec as P

LAGS = 1024
AXES = ("tm", "sta")
ROWS, CORES, LAYERS, COLUMNS = 2, 2, 4, 2
BLOCK = 128
FIRST_BINS = 512


def lag_table(bins, lags):
    bin_index = jnp.arange(bins, dtype=jnp.int32)[:, None]
    lag_index = jnp.arange(lags, dtype=jnp.int32)[None, :] - lags // 2
    phase = (bin_index * lag_index % (2 * bins)).astype(jnp.float32) * (jnp.pi / bins)
    scale = 1.0 / bins**0.5
    return jnp.concatenate([jnp.cos(phase) * scale, -jnp.sin(phase) * scale], axis=0)


def cross_spectra(first, second, bins):
    first = first.astype(jnp.float32)
    second = second.astype(jnp.float32)
    real_a, imag_a = (first[..., :bins], first[..., bins:])
    real_b, imag_b = (second[..., :bins], second[..., bins:])
    real_c = real_a * real_b + imag_a * imag_b
    imag_c = real_a * imag_b - imag_a * real_b
    return jnp.concatenate([real_c, imag_c], axis=-1)


def local_any_size(spectra, pair_list, pair_stations, owner_code):
    local_spectra = spectra[0]
    width = local_spectra.shape[1]
    bins = width // 2
    catalogue = pair_stations.shape[1]
    groups = lax.axis_size("tm")
    capacity = 2 * catalogue // groups
    listed = pair_list[0, 0]
    first_station = pair_stations[0][listed]
    second_station = pair_stations[1][listed]
    codes = owner_code[listed]
    table = lag_table(bins, LAGS)
    all_spectra = lax.all_gather(local_spectra, "sta", axis=0, tiled=True)
    first = all_spectra[first_station]
    second = all_spectra[second_station]
    cross = cross_spectra(first, second, bins)
    partial_lags = jnp.dot(
        cross, table, precision=lax.Precision.HIGHEST, preferred_element_type=jnp.float32
    )
    slots = jnp.arange(capacity * lax.axis_size("tm"), dtype=jnp.int32)
    select = (slots[:, None] == codes[None, :]).astype(jnp.float32)
    return lax.psum_scatter(
        jnp.dot(
            select,
            partial_lags,
            precision=lax.Precision.HIGHEST,
            preferred_element_type=jnp.float32,
        ),
        "tm",
        scatter_dimension=0,
        tiled=True,
    )


def moves(target):
    def place(row, core, layer, column):
        return (row * CORES + core) * LAYERS * COLUMNS + layer * COLUMNS + column

    return [
        (place(row, core, layer, column), place(*target(row, core, layer, column)))
        for row in range(ROWS)
        for core in range(CORES)
        for layer in range(LAYERS)
        for column in range(COLUMNS)
    ]


OTHER_ROW = moves(lambda r, c, z, x: (1 - r, c, z, x))
OTHER_CORE = moves(lambda r, c, z, x: (r, 1 - c, z, x))
FIRST_SIDE = moves(lambda r, c, z, x: (r, c, z, 1 - x) if c == 0 else (1 - r, c, z, x))
SECOND_SIDE = moves(lambda r, c, z, x: (1 - r, c, z, x) if c == 0 else (r, c, z, 1 - x))


def layer_turn(step):
    return moves(lambda r, c, z, x: (r, c, (z + step) % LAYERS, x))


def send(value, pairs):
    return lax.ppermute(value, AXES, pairs)


def split_table(bins, start, stop):
    index = np.arange(bins)[:, None] * (np.arange(LAGS)[None, :] - LAGS // 2) % (2 * bins)
    angle = index * (np.pi / bins)
    both = np.stack([np.cos(angle), -np.sin(angle)]) / np.sqrt(bins)
    rows = both[:, start:stop].reshape(2, -1, BLOCK, LAGS).transpose(1, 0, 2, 3).reshape(-1, LAGS)
    rows = rows.astype(np.float32)
    high = rows.astype(jnp.bfloat16)
    low = (rows - high.astype(np.float32)).astype(jnp.bfloat16)
    return jnp.asarray(high), jnp.asarray(low)


def chunk_kernel(final, core_ref, picks_ref, *refs):
    tops, rests, refs = refs[:8], refs[8:12], refs[12:]
    high_ref, low_ref, refs = refs[0], refs[1], refs[2:]
    if final:
        earlier_ref, select_ref, theirs_ref, ours_ref, high_cross, low_cross, total_ref = refs
    else:
        total_ref, high_cross, low_cross = refs
    step = pl.program_id(0)
    entries = picks_ref.shape[1] // 2

    def block(side):
        top = jnp.concatenate([tops[2 * side][...], tops[2 * side + 1][...]], axis=1)
        return jnp.concatenate([top, rests[side][...]], axis=0)

    def cross(order):
        for segment in range(2):
            same, other = order[2 * segment], order[2 * segment + 1]
            stations = jnp.concatenate([block(same), block(other)], axis=0)
            both = jnp.dot(picks_ref[segment], stations, preferred_element_type=jnp.float32)
            real_a, imag_a = both[:entries, :BLOCK], both[:entries, BLOCK:]
            real_b, imag_b = both[entries:, :BLOCK], both[entries:, BLOCK:]
            value = jnp.concatenate(
                [real_a * real_b + imag_a * imag_b, real_a * imag_b - imag_a * real_b], axis=1
            )
            high = value.astype(jnp.bfloat16)
            rows = pl.ds(segment * entries, entries)
            high_cross[rows, :] = high
            low_cross[rows, :] = (value - high.astype(jnp.float32)).astype(jnp.bfloat16)

    @pl.when(core_ref[0] == 0)
    def _():
        cross((0, 1, 2, 3))

    @pl.when(core_ref[0] == 1)
    def _():
        cross((0, 2, 1, 3))

    lags = jnp.dot(high_cross[...], high_ref[...], preferred_element_type=jnp.float32)
    lags += jnp.dot(low_cross[...], high_ref[...], preferred_element_type=jnp.float32)
    lags += jnp.dot(high_cross[...], low_ref[...], preferred_element_type=jnp.float32)

    @pl.when(step == 0)
    def _():
        total_ref[...] = (earlier_ref[...] + lags) if final else lags

    @pl.when(step > 0)
    def _():
        total_ref[...] += lags

    if final:

        @pl.when(step == pl.num_programs(0) - 1)
        def _():
            total = total_ref[...]
            high = total.astype(jnp.bfloat16)
            low = (total - high.astype(jnp.float32)).astype(jnp.bfloat16)
            for part, out_ref in enumerate((theirs_ref, ours_ref)):
                out_ref[...] = jnp.dot(
                    select_ref[part], high, preferred_element_type=jnp.float32
                ) + jnp.dot(select_ref[part], low, preferred_element_type=jnp.float32)


def correlate_chunk(core, picks, own, tops, rests, start, stop, bins, earlier=None, select=None):
    final = earlier is not None
    steps = (stop - start) // BLOCK
    first_block = start // BLOCK
    stations = own.shape[0]
    entries = picks.shape[1]
    high, low = split_table(bins, start, stop)
    whole = lambda shape: pl.BlockSpec(shape, lambda j, c: (0,) * len(shape))
    real = pl.BlockSpec((stations, BLOCK), lambda j, c: (0, first_block + j))
    imag = pl.BlockSpec((stations, BLOCK), lambda j, c: (0, bins // BLOCK + first_block + j))
    rest = pl.BlockSpec((rests[0].shape[0], 2 * BLOCK), lambda j, c: (0, j))
    table = pl.BlockSpec((2 * BLOCK, LAGS), lambda j, c: (j, 0))
    operands = [picks, *(t for t in tops for _ in range(2)), *rests, high, low]
    in_specs = [whole(picks.shape), *([real, imag] * 4), *([rest] * 4), table, table]
    scratch = [
        pltpu.VMEM((entries, 2 * BLOCK), jnp.bfloat16),
        pltpu.VMEM((entries, 2 * BLOCK), jnp.bfloat16),
    ]
    out_shape = [jax.ShapeDtypeStruct((entries, LAGS), jnp.float32)]
    if final:
        operands += [earlier, select]
        in_specs += [whole(earlier.shape), whole(select.shape)]
        out_shape = [jax.ShapeDtypeStruct((select.shape[1], LAGS), jnp.float32)] * 2
        scratch.append(pltpu.VMEM((entries, LAGS), jnp.float32))
    result = pl.pallas_call(
        functools.partial(chunk_kernel, final),
        out_shape=out_shape,
        grid_spec=pltpu.PrefetchScalarGridSpec(
            num_scalar_prefetch=1,
            grid=(steps,),
            in_specs=in_specs,
            out_specs=[whole(o.shape) for o in out_shape],
            scratch_shapes=scratch,
        ),
        compiler_params=pltpu.CompilerParams(vmem_limit_bytes=40 * 1024 * 1024),
        cost_estimate=pl.CostEstimate(
            flops=2 * entries * (stop - start) * 2 * (3 * LAGS + entries),
            bytes_accessed=(stop - start) * 2 * (4 * LAGS + 16 * stations * 2),
            transcendentals=0,
        ),
        name="correlate_last" if final else "correlate",
    )(core, *operands)
    return result


def local_grid(spectra, pair_list, pair_stations, owner_code):
    own = spectra[0]
    stations, width = own.shape
    bins = width // 2
    catalogue = pair_stations.shape[1]
    capacity = 2 * catalogue // (ROWS * CORES)
    row, core = lax.axis_index("tm") // CORES, lax.axis_index("tm") % CORES
    layer, column = lax.axis_index("sta") // COLUMNS, lax.axis_index("sta") % COLUMNS

    listed_here = pair_list[0, 0]
    first_own = send(own, FIRST_SIDE)
    second_own = send(own, SECOND_SIDE)
    listed_there = send(listed_here, OTHER_ROW)
    cuts = [(0, FIRST_BINS), (FIRST_BINS, bins)]
    turned = []
    for start, stop in cuts:
        blocks = own.reshape(stations, 2, bins // BLOCK, BLOCK)[:, :, start // BLOCK : stop // BLOCK]
        part = blocks.transpose(0, 2, 1, 3).reshape(stations, 2 * (stop - start))
        turned.append(
            jnp.concatenate([send(part, layer_turn(step)) for step in range(1, LAYERS)], axis=0)
        )
    diagonal_own = send(first_own, SECOND_SIDE)
    tops = (own, first_own, second_own, diagonal_own)
    rests = []
    for part in turned:
        first, second = send(part, FIRST_SIDE), send(part, SECOND_SIDE)
        rests.append((part, first, second, send(first, SECOND_SIDE)))

    listed = jnp.stack([listed_here, listed_there])
    hit = listed[:, :, None] == jnp.arange(catalogue, dtype=jnp.int32)
    look_up = lambda values: jnp.sum(jnp.where(hit, values, 0), axis=-1)
    pair = jnp.concatenate([look_up(pair_stations[0]), look_up(pair_stations[1])], axis=1)
    holder, place = pair // stations, pair % stations
    turn = (layer - holder // COLUMNS) % LAYERS
    beside = (holder % COLUMNS) ^ column
    position = (beside * LAYERS + turn) * stations + place
    spots = jnp.arange(COLUMNS * LAYERS * stations, dtype=jnp.int32)
    picks = (position[:, :, None] == spots).astype(jnp.bfloat16)
    codes = look_up(owner_code).reshape(-1)
    owner = row * CORES + jnp.stack([1 - core, core])
    slots = owner[:, None] * capacity + jnp.arange(capacity, dtype=jnp.int32)
    select = (slots[:, :, None] == codes).astype(jnp.bfloat16)

    core = core.astype(jnp.int32).reshape(1)
    (early,) = correlate_chunk(core, picks, own, tops, rests[0], *cuts[0], bins)
    theirs, ours = correlate_chunk(
        core, picks, own, tops, rests[1], *cuts[1], bins, earlier=early, select=select
    )
    return ours + send(theirs, OTHER_CORE)


def solution(mesh):
    sizes = (mesh.shape["tm"], mesh.shape["sta"])
    fits = sizes == (ROWS * CORES, LAYERS * COLUMNS)
    return jax.shard_map(
        local_grid if fits else local_any_size,
        mesh=mesh,
        in_specs=(P("tm", "sta", None), P("tm", "sta", None), P(None, "sta"), P("sta")),
        out_specs=P(("tm", "sta"), None),
        check_vma=False,
    )
```

```python
import functools

import jax
import jax.numpy as jnp
import numpy as np
from jax import lax
from jax.experimental import pallas as pl
from jax.experimental.pallas import tpu as pltpu
from jax.sharding import PartitionSpec as P

LAGS = 1024
AXES = ("tm", "sta")
ROWS, CORES, LAYERS, COLUMNS = 2, 2, 4, 2
BLOCK = 256
FIRST_BINS = 512


def lag_table(bins, lags):
    bin_index = jnp.arange(bins, dtype=jnp.int32)[:, None]
    lag_index = jnp.arange(lags, dtype=jnp.int32)[None, :] - lags // 2
    phase = (bin_index * lag_index % (2 * bins)).astype(jnp.float32) * (jnp.pi / bins)
    scale = 1.0 / bins**0.5
    return jnp.concatenate([jnp.cos(phase) * scale, -jnp.sin(phase) * scale], axis=0)


def cross_spectra(first, second, bins):
    first = first.astype(jnp.float32)
    second = second.astype(jnp.float32)
    real_a, imag_a = (first[..., :bins], first[..., bins:])
    real_b, imag_b = (second[..., :bins], second[..., bins:])
    real_c = real_a * real_b + imag_a * imag_b
    imag_c = real_a * imag_b - imag_a * real_b
    return jnp.concatenate([real_c, imag_c], axis=-1)


def local_any_size(spectra, pair_list, pair_stations, owner_code):
    local_spectra = spectra[0]
    width = local_spectra.shape[1]
    bins = width // 2
    catalogue = pair_stations.shape[1]
    groups = lax.axis_size("tm")
    capacity = 2 * catalogue // groups
    listed = pair_list[0, 0]
    first_station = pair_stations[0][listed]
    second_station = pair_stations[1][listed]
    codes = owner_code[listed]
    table = lag_table(bins, LAGS)
    all_spectra = lax.all_gather(local_spectra, "sta", axis=0, tiled=True)
    first = all_spectra[first_station]
    second = all_spectra[second_station]
    cross = cross_spectra(first, second, bins)
    partial_lags = jnp.dot(
        cross, table, precision=lax.Precision.HIGHEST, preferred_element_type=jnp.float32
    )
    slots = jnp.arange(capacity * lax.axis_size("tm"), dtype=jnp.int32)
    select = (slots[:, None] == codes[None, :]).astype(jnp.float32)
    return lax.psum_scatter(
        jnp.dot(
            select,
            partial_lags,
            precision=lax.Precision.HIGHEST,
            preferred_element_type=jnp.float32,
        ),
        "tm",
        scatter_dimension=0,
        tiled=True,
    )


def moves(target):
    def place(row, core, layer, column):
        return (row * CORES + core) * LAYERS * COLUMNS + layer * COLUMNS + column

    return [
        (place(row, core, layer, column), place(*target(row, core, layer, column)))
        for row in range(ROWS)
        for core in range(CORES)
        for layer in range(LAYERS)
        for column in range(COLUMNS)
    ]


OTHER_ROW = moves(lambda r, c, z, x: (1 - r, c, z, x))
OTHER_CORE = moves(lambda r, c, z, x: (r, 1 - c, z, x))
OTHER_COLUMN = moves(lambda r, c, z, x: (r, c, z, 1 - x))
DIAGONAL = moves(lambda r, c, z, x: (1 - r, c, z, x) if c == 0 else (r, c, z, 1 - x))


def layer_turn(step):
    return moves(lambda r, c, z, x: (r, c, (z + step) % LAYERS, x))


def send(value, pairs):
    return lax.ppermute(value, AXES, pairs)


def split_table(bins, start, stop):
    index = np.arange(bins)[:, None] * (np.arange(LAGS)[None, :] - LAGS // 2) % (2 * bins)
    angle = index * (np.pi / bins)
    both = np.stack([np.cos(angle), -np.sin(angle)]) / np.sqrt(bins)
    rows = both[:, start:stop].reshape(-1, LAGS).astype(np.float32)
    high = rows.astype(jnp.bfloat16)
    low = (rows - high.astype(np.float32)).astype(jnp.bfloat16)
    return jnp.asarray(high), jnp.asarray(low)


def two_parts(value):
    high = value.astype(jnp.bfloat16)
    return high, (value - high.astype(jnp.float32)).astype(jnp.bfloat16)


def chunk_kernel(final, start, bins, picks_ref, *refs):
    tops, rests, refs = refs[:4], refs[4:8], refs[8:]
    table_high, table_low, refs = refs[0], refs[1], refs[2:]
    if final:
        earlier_ref, select_ref, theirs_ref, ours_ref, high_cross, low_cross = refs
    else:
        total_ref, high_cross, low_cross = refs
    entries = picks_ref.shape[1] // 2
    chunk = rests[0].shape[1] // 2

    for segment in range(2):
        rows = slice(segment * entries, (segment + 1) * entries)
        for at in range(0, chunk, BLOCK):
            blocks = []
            for side in (2 * segment, 2 * segment + 1):
                for ref, real in ((tops[side], start + at), (rests[side], at)):
                    imag = real + (bins if ref is tops[side] else chunk)
                    blocks.append(
                        jnp.concatenate(
                            [ref[:, real : real + BLOCK], ref[:, imag : imag + BLOCK]], axis=1
                        )
                    )
            stations = jnp.concatenate(blocks, axis=0)
            both = jnp.dot(picks_ref[segment], stations, preferred_element_type=jnp.float32)
            real_a, imag_a = both[:entries, :BLOCK], both[:entries, BLOCK:]
            real_b, imag_b = both[entries:, :BLOCK], both[entries:, BLOCK:]
            for value, column in (
                (real_a * real_b + imag_a * imag_b, at),
                (real_a * imag_b - imag_a * real_b, chunk + at),
            ):
                columns = slice(column, column + BLOCK)
                high_cross[rows, columns], low_cross[rows, columns] = two_parts(value)

    dot = functools.partial(jnp.dot, preferred_element_type=jnp.float32)
    lags = dot(high_cross[...], table_high[...])
    lags += dot(low_cross[...], table_high[...])
    lags += dot(high_cross[...], table_low[...])
    if final:
        high, low = two_parts(earlier_ref[...] + lags)
        for part, out_ref in enumerate((theirs_ref, ours_ref)):
            out_ref[...] = dot(select_ref[part], high) + dot(select_ref[part], low)
    else:
        total_ref[...] = lags


def correlate_chunk(picks, tops, rests, start, stop, bins, earlier=None, select=None):
    final = earlier is not None
    entries = picks.shape[1]
    operands = [picks, *tops, *rests, *split_table(bins, start, stop)]
    out_shape = [jax.ShapeDtypeStruct((entries, LAGS), jnp.float32)]
    if final:
        operands += [earlier, select]
        out_shape = [jax.ShapeDtypeStruct((select.shape[1], LAGS), jnp.float32)] * 2
    in_vmem = pl.BlockSpec(memory_space=pltpu.VMEM)
    return pl.pallas_call(
        functools.partial(chunk_kernel, final, start, bins),
        out_shape=out_shape,
        in_specs=[in_vmem] * len(operands),
        out_specs=[in_vmem] * len(out_shape),
        scratch_shapes=[pltpu.VMEM((entries, 2 * (stop - start)), jnp.bfloat16)] * 2,
        compiler_params=pltpu.CompilerParams(vmem_limit_bytes=24 * 1024 * 1024),
        cost_estimate=pl.CostEstimate(
            flops=2 * entries * (stop - start) * 2 * (3 * LAGS + entries),
            bytes_accessed=(stop - start) * 2 * (4 * LAGS + 16 * tops[0].shape[0] * 2),
            transcendentals=0,
        ),
        name="correlate_last" if final else "correlate",
    )(*operands)


def local_grid(spectra, pair_list, pair_stations, owner_code):
    own = spectra[0]
    stations, width = own.shape
    bins = width // 2
    catalogue = pair_stations.shape[1]
    capacity = 2 * catalogue // (ROWS * CORES)
    row, core = lax.axis_index("tm") // CORES, lax.axis_index("tm") % CORES
    layer, column = lax.axis_index("sta") // COLUMNS, lax.axis_index("sta") % COLUMNS
    after = lambda value, *others: lax.optimization_barrier((value, *others))[0]

    def around(value, *others):
        side = send(value, OTHER_COLUMN)
        ahead = send(value, OTHER_ROW)
        return side, ahead

    def diagonal(side, ahead, *others):
        forwarded = after(jnp.where(core == 0, side, ahead), *others)
        return send(forwarded, DIAGONAL)

    def turn(value):
        return [send(value, layer_turn(step)) for step in (2, 1, 3)]

    def chunk(start, stop):
        return jnp.concatenate([own[:, start:stop], own[:, bins + start : bins + stop]], axis=1)

    listed_here = pair_list[0, 0]
    cuts = [(0, FIRST_BINS), (FIRST_BINS, bins)]
    side_own, ahead_own = around(own)
    turned_first = turn(chunk(*cuts[0]))
    diagonal_own = diagonal(side_own, ahead_own)
    listed_there = send(after(listed_here, side_own, ahead_own), OTHER_ROW)
    turned_last = turn(after(chunk(*cuts[1]), side_own, ahead_own))
    rest = after(jnp.concatenate(turned_first, axis=0), diagonal_own)
    side, ahead = around(rest)
    first_rests = (rest, side, ahead, diagonal(side, ahead))
    rest = after(jnp.concatenate(turned_last, axis=0), side, ahead)
    side, ahead = around(rest)
    tops = (own, side_own, ahead_own, diagonal_own)

    listed = jnp.stack([listed_here, listed_there])
    hit = listed[:, :, None] == jnp.arange(catalogue, dtype=jnp.int32)
    look_up = lambda values: jnp.sum(jnp.where(hit, values, 0), axis=-1)
    pair = jnp.concatenate([look_up(pair_stations[0]), look_up(pair_stations[1])], axis=1)
    holder, place = pair // stations, pair % stations
    turns = (layer - holder // COLUMNS) % LAYERS
    turns = jnp.where(turns == 2, 1, jnp.where(turns == 1, 2, turns))
    beside = (holder % COLUMNS) ^ column
    position = (beside * LAYERS + turns) * stations + place
    spots = jnp.arange(COLUMNS * LAYERS * stations, dtype=jnp.int32)
    picks = (position[:, :, None] == spots).astype(jnp.bfloat16)
    codes = look_up(owner_code).reshape(-1)
    owner = row * CORES + jnp.stack([1 - core, core])
    slots = owner[:, None] * capacity + jnp.arange(capacity, dtype=jnp.int32)
    select = (slots[:, :, None] == codes).astype(jnp.bfloat16)

    (early,) = correlate_chunk(picks, tops, first_rests, *cuts[0], bins)
    last_rests = (rest, side, ahead, diagonal(side, ahead))
    theirs, ours = correlate_chunk(
        picks, tops, last_rests, *cuts[1], bins, earlier=early, select=select
    )
    return ours + send(theirs, OTHER_CORE)


def solution(mesh):
    sizes = (mesh.shape["tm"], mesh.shape["sta"])
    fits = sizes == (ROWS * CORES, LAYERS * COLUMNS)
    return jax.shard_map(
        local_grid if fits else local_any_size,
        mesh=mesh,
        in_specs=(P("tm", "sta", None), P("tm", "sta", None), P(None, "sta"), P("sta")),
        out_specs=P(("tm", "sta"), None),
        check_vma=False,
    )
```

```python
import functools

import jax
import jax.numpy as jnp
import numpy as np
from jax import lax
from jax.experimental import pallas as pl
from jax.experimental.pallas import tpu as pltpu
from jax.sharding import PartitionSpec as P

LAGS = 1024
AXES = ("tm", "sta")
ROWS, CORES, LAYERS, COLUMNS = 2, 2, 4, 2
BLOCK = 256


def lag_table(bins, lags):
    bin_index = jnp.arange(bins, dtype=jnp.int32)[:, None]
    lag_index = jnp.arange(lags, dtype=jnp.int32)[None, :] - lags // 2
    phase = (bin_index * lag_index % (2 * bins)).astype(jnp.float32) * (jnp.pi / bins)
    scale = 1.0 / bins**0.5
    return jnp.concatenate([jnp.cos(phase) * scale, -jnp.sin(phase) * scale], axis=0)


def cross_spectra(first, second, bins):
    first = first.astype(jnp.float32)
    second = second.astype(jnp.float32)
    real_a, imag_a = (first[..., :bins], first[..., bins:])
    real_b, imag_b = (second[..., :bins], second[..., bins:])
    real_c = real_a * real_b + imag_a * imag_b
    imag_c = real_a * imag_b - imag_a * real_b
    return jnp.concatenate([real_c, imag_c], axis=-1)


def local_any_size(spectra, pair_list, pair_stations, owner_code):
    local_spectra = spectra[0]
    width = local_spectra.shape[1]
    bins = width // 2
    catalogue = pair_stations.shape[1]
    groups = lax.axis_size("tm")
    capacity = 2 * catalogue // groups
    listed = pair_list[0, 0]
    first_station = pair_stations[0][listed]
    second_station = pair_stations[1][listed]
    codes = owner_code[listed]
    table = lag_table(bins, LAGS)
    all_spectra = lax.all_gather(local_spectra, "sta", axis=0, tiled=True)
    first = all_spectra[first_station]
    second = all_spectra[second_station]
    cross = cross_spectra(first, second, bins)
    partial_lags = jnp.dot(
        cross, table, precision=lax.Precision.HIGHEST, preferred_element_type=jnp.float32
    )
    slots = jnp.arange(capacity * lax.axis_size("tm"), dtype=jnp.int32)
    select = (slots[:, None] == codes[None, :]).astype(jnp.float32)
    return lax.psum_scatter(
        jnp.dot(
            select,
            partial_lags,
            precision=lax.Precision.HIGHEST,
            preferred_element_type=jnp.float32,
        ),
        "tm",
        scatter_dimension=0,
        tiled=True,
    )


def moves(target):
    def place(row, core, layer, column):
        return (row * CORES + core) * LAYERS * COLUMNS + layer * COLUMNS + column

    return [
        (place(row, core, layer, column), place(*to))
        for row in range(ROWS)
        for core in range(CORES)
        for layer in range(LAYERS)
        for column in range(COLUMNS)
        if (to := target(row, core, layer, column)) is not None
    ]


OTHER_ROW = moves(lambda r, c, z, x: (1 - r, c, z, x))
OTHER_CORE = moves(lambda r, c, z, x: (r, 1 - c, z, x))
OTHER_COLUMN = moves(lambda r, c, z, x: (r, c, z, 1 - x))
DIAGONAL = moves(lambda r, c, z, x: (1 - r, c, z, x) if c == 0 else (r, c, z, 1 - x))
PAIR_SWAP = moves(lambda r, c, z, x: (r, c, z ^ 1, x))
INNER_SWAP = moves(lambda r, c, z, x: (r, c, 3 - z, x) if z in (1, 2) else None)
OUTWARD = moves(lambda r, c, z, x: (r, c, z ^ 1, x) if z in (1, 2) else None)


def send(value, pairs):
    return lax.ppermute(value, AXES, pairs)


def split_table(bins):
    index = np.arange(bins)[:, None] * (np.arange(LAGS)[None, :] - LAGS // 2) % (2 * bins)
    angle = index * (np.pi / bins)
    rows = np.concatenate([np.cos(angle), -np.sin(angle)]) / np.sqrt(bins)
    rows = rows.astype(np.float32)
    high = rows.astype(jnp.bfloat16)
    low = (rows - high.astype(np.float32)).astype(jnp.bfloat16)
    return jnp.asarray(high), jnp.asarray(low)


def two_parts(value):
    high = value.astype(jnp.bfloat16)
    return high, (value - high.astype(jnp.float32)).astype(jnp.bfloat16)


def segment_kernel(picks_ref, select_ref, table_high, table_low, *refs):
    blocks, refs = refs[: 2 * LAYERS], refs[2 * LAYERS :]
    earlier, (theirs_ref, ours_ref, high_cross, low_cross) = refs[:-4], refs[-4:]
    entries = picks_ref.shape[0] // 2
    bins = table_high.shape[0] // 2
    dot = functools.partial(jnp.dot, preferred_element_type=jnp.float32)

    for at in range(0, bins, BLOCK):
        real, imag = slice(at, at + BLOCK), slice(bins + at, bins + at + BLOCK)
        stations = jnp.concatenate(
            [jnp.concatenate([ref[:, real], ref[:, imag]], axis=1) for ref in blocks], axis=0
        )
        both = dot(picks_ref[...], stations)
        real_a, imag_a = both[:entries, :BLOCK], both[:entries, BLOCK:]
        real_b, imag_b = both[entries:, :BLOCK], both[entries:, BLOCK:]
        for value, columns in (
            (real_a * real_b + imag_a * imag_b, real),
            (real_a * imag_b - imag_a * real_b, imag),
        ):
            high_cross[:, columns], low_cross[:, columns] = two_parts(value)

    lags = dot(high_cross[...], table_high[...])
    lags += dot(low_cross[...], table_high[...])
    lags += dot(high_cross[...], table_low[...])
    high, low = two_parts(lags)
    for part, out_ref in enumerate((theirs_ref, ours_ref)):
        slots = dot(select_ref[part], high) + dot(select_ref[part], low)
        out_ref[...] = slots + earlier[part][...] if earlier else slots


def add_segment(picks, select, table, blocks, earlier=()):
    entries, (_, slots, _) = picks.shape[0] // 2, select.shape
    bins = table[0].shape[0] // 2
    operands = [picks, select, *table, *blocks, *earlier]
    in_vmem = pl.BlockSpec(memory_space=pltpu.VMEM)
    return pl.pallas_call(
        segment_kernel,
        out_shape=[jax.ShapeDtypeStruct((slots, LAGS), jnp.float32)] * 2,
        in_specs=[in_vmem] * len(operands),
        out_specs=[in_vmem] * 2,
        scratch_shapes=[pltpu.VMEM((entries, 2 * bins), jnp.bfloat16)] * 2,
        compiler_params=pltpu.CompilerParams(vmem_limit_bytes=24 * 1024 * 1024),
        cost_estimate=pl.CostEstimate(
            flops=4 * entries * (bins * (3 * LAGS + 2 * picks.shape[1]) + 2 * slots * LAGS),
            bytes_accessed=8 * bins * (LAGS + picks.shape[1]),
            transcendentals=0,
        ),
        name="add_segment",
    )(*operands)


def local_grid(spectra, pair_list, pair_stations, owner_code):
    own = spectra[0]
    stations, width = own.shape
    bins = width // 2
    catalogue = pair_stations.shape[1]
    capacity = 2 * catalogue // (ROWS * CORES)
    row, core = lax.axis_index("tm") // CORES, lax.axis_index("tm") % CORES
    layer, column = lax.axis_index("sta") // COLUMNS, lax.axis_index("sta") % COLUMNS
    after = lambda value, *others: lax.optimization_barrier((value, *others))[0]

    def around(value):
        return send(value, OTHER_COLUMN), send(value, OTHER_ROW)

    def diagonal(side, ahead):
        return send(jnp.where(core == 0, side, ahead), DIAGONAL)

    inner = (layer == 1) | (layer == 2)
    side, ahead = around(own)
    near, swapped = send(own, PAIR_SWAP), send(own, INNER_SWAP)
    corner = diagonal(side, ahead)
    near_side, near_ahead = around(after(near, side, ahead))
    third = jnp.where(inner, swapped, send(swapped, OUTWARD))
    swapped = send(near, INNER_SWAP)
    fourth = jnp.where(inner, swapped, send(swapped, OUTWARD))
    listed_here = pair_list[0, 0]
    listed_there = send(after(listed_here, corner), OTHER_ROW)

    listed = jnp.stack([listed_here, listed_there])
    hit = listed[:, :, None] == jnp.arange(catalogue, dtype=jnp.int32)
    look_up = lambda values: jnp.sum(jnp.where(hit, values, 0), axis=-1)
    pair = jnp.concatenate([look_up(pair_stations[0]), look_up(pair_stations[1])], axis=1)
    holder, place = pair // stations, pair % stations
    apart = layer ^ (holder // COLUMNS)
    turns = jnp.where((apart > 1) & inner, 5 - apart, apart)
    beside = (holder % COLUMNS) ^ column
    position = (beside * LAYERS + turns) * stations + place
    spots = jnp.arange(COLUMNS * LAYERS * stations, dtype=jnp.int32)
    picks = (position[:, :, None] == spots).astype(jnp.bfloat16)

    third_side, third_ahead = around(after(third, corner))
    near_corner = diagonal(near_side, near_ahead)
    fourth_side, fourth_ahead = around(after(fourth, picks))
    third_corner = diagonal(third_side, third_ahead)
    fourth_corner = diagonal(fourth_side, fourth_ahead)
    here = (own, near, third, fourth, side, near_side, third_side, fourth_side)
    there = (ahead, near_ahead, third_ahead, fourth_ahead)
    there += (corner, near_corner, third_corner, fourth_corner)

    codes = look_up(owner_code)
    owner = row * CORES + jnp.stack([1 - core, core])
    slots = owner[:, None] * capacity + jnp.arange(capacity, dtype=jnp.int32)
    select = (slots[:, :, None] == codes[:, None, None, :]).astype(jnp.bfloat16)

    table = split_table(bins)
    sums = add_segment(picks[0], select[0], table, here)
    theirs, ours = add_segment(picks[1], select[1], table, there, sums)
    return ours + send(theirs, OTHER_CORE)


def solution(mesh):
    sizes = (mesh.shape["tm"], mesh.shape["sta"])
    fits = sizes == (ROWS * CORES, LAYERS * COLUMNS)
    return jax.shard_map(
        local_grid if fits else local_any_size,
        mesh=mesh,
        in_specs=(P("tm", "sta", None), P("tm", "sta", None), P(None, "sta"), P("sta")),
        out_specs=P(("tm", "sta"), None),
        check_vma=False,
    )
```

```python
import functools

import jax
import jax.numpy as jnp
import numpy as np
from jax import lax
from jax.experimental import pallas as pl
from jax.experimental.pallas import tpu as pltpu
from jax.sharding import PartitionSpec as P

LAGS = 1024
AXES = ("tm", "sta")
ROWS, CORES, LAYERS, COLUMNS = 2, 2, 4, 2
BLOCK = 256


def lag_table(bins, lags):
    bin_index = jnp.arange(bins, dtype=jnp.int32)[:, None]
    lag_index = jnp.arange(lags, dtype=jnp.int32)[None, :] - lags // 2
    phase = (bin_index * lag_index % (2 * bins)).astype(jnp.float32) * (jnp.pi / bins)
    scale = 1.0 / bins**0.5
    return jnp.concatenate([jnp.cos(phase) * scale, -jnp.sin(phase) * scale], axis=0)


def cross_spectra(first, second, bins):
    first = first.astype(jnp.float32)
    second = second.astype(jnp.float32)
    real_a, imag_a = (first[..., :bins], first[..., bins:])
    real_b, imag_b = (second[..., :bins], second[..., bins:])
    real_c = real_a * real_b + imag_a * imag_b
    imag_c = real_a * imag_b - imag_a * real_b
    return jnp.concatenate([real_c, imag_c], axis=-1)


def local_any_size(spectra, pair_list, pair_stations, owner_code):
    local_spectra = spectra[0]
    width = local_spectra.shape[1]
    bins = width // 2
    catalogue = pair_stations.shape[1]
    groups = lax.axis_size("tm")
    capacity = 2 * catalogue // groups
    listed = pair_list[0, 0]
    first_station = pair_stations[0][listed]
    second_station = pair_stations[1][listed]
    codes = owner_code[listed]
    table = lag_table(bins, LAGS)
    all_spectra = lax.all_gather(local_spectra, "sta", axis=0, tiled=True)
    first = all_spectra[first_station]
    second = all_spectra[second_station]
    cross = cross_spectra(first, second, bins)
    partial_lags = jnp.dot(
        cross, table, precision=lax.Precision.HIGHEST, preferred_element_type=jnp.float32
    )
    slots = jnp.arange(capacity * lax.axis_size("tm"), dtype=jnp.int32)
    select = (slots[:, None] == codes[None, :]).astype(jnp.float32)
    return lax.psum_scatter(
        jnp.dot(
            select,
            partial_lags,
            precision=lax.Precision.HIGHEST,
            preferred_element_type=jnp.float32,
        ),
        "tm",
        scatter_dimension=0,
        tiled=True,
    )


def moves(target):
    def place(row, core, layer, column):
        return (row * CORES + core) * LAYERS * COLUMNS + layer * COLUMNS + column

    return [
        (place(row, core, layer, column), place(*to))
        for row in range(ROWS)
        for core in range(CORES)
        for layer in range(LAYERS)
        for column in range(COLUMNS)
        if (to := target(row, core, layer, column)) is not None
    ]


OTHER_ROW = moves(lambda r, c, z, x: (1 - r, c, z, x))
OTHER_CORE = moves(lambda r, c, z, x: (r, 1 - c, z, x))
OTHER_COLUMN = moves(lambda r, c, z, x: (r, c, z, 1 - x))
DIAGONAL = moves(lambda r, c, z, x: (1 - r, c, z, x) if c == 0 else (r, c, z, 1 - x))
PAIR_SWAP = moves(lambda r, c, z, x: (r, c, z ^ 1, x))
INNER_SWAP = moves(lambda r, c, z, x: (r, c, 3 - z, x) if z in (1, 2) else (r, 1 - c, z, x))
OUTWARD = PAIR_SWAP


def send(value, pairs):
    return lax.ppermute(value, AXES, pairs)


def split_table(bins):
    index = np.arange(bins)[:, None] * (np.arange(LAGS)[None, :] - LAGS // 2) % (2 * bins)
    angle = index * (np.pi / bins)
    rows = np.concatenate([np.cos(angle), -np.sin(angle)]) / np.sqrt(bins)
    rows = rows.astype(np.float32)
    high = rows.astype(jnp.bfloat16)
    low = (rows - high.astype(np.float32)).astype(jnp.bfloat16)
    return jnp.asarray(high), jnp.asarray(low)


def two_parts(value):
    high = value.astype(jnp.bfloat16)
    return high, (value - high.astype(jnp.float32)).astype(jnp.bfloat16)


def segment_kernel(picks_ref, select_ref, table_high, table_low, *refs):
    blocks, refs = refs[:6], refs[6:]
    earlier, (theirs_ref, ours_ref, high_cross, low_cross) = refs[:-4], refs[-4:]
    entries = picks_ref.shape[0] // 2
    bins = table_high.shape[0] // 2
    dot = functools.partial(jnp.dot, preferred_element_type=jnp.float32)

    for at in range(0, bins, BLOCK):
        real, imag = slice(at, at + BLOCK), slice(bins + at, bins + at + BLOCK)
        stations = jnp.concatenate(
            [jnp.concatenate([ref[:, real], ref[:, imag]], axis=1) for ref in blocks], axis=0
        )
        both = dot(picks_ref[...], stations)
        real_a, imag_a = both[:entries, :BLOCK], both[:entries, BLOCK:]
        real_b, imag_b = both[entries:, :BLOCK], both[entries:, BLOCK:]
        for value, columns in (
            (real_a * real_b + imag_a * imag_b, real),
            (real_a * imag_b - imag_a * real_b, imag),
        ):
            high_cross[:, columns], low_cross[:, columns] = two_parts(value)

    lags = dot(high_cross[...], table_high[...])
    lags += dot(low_cross[...], table_high[...])
    lags += dot(high_cross[...], table_low[...])
    high, low = two_parts(lags)
    for part, out_ref in enumerate((theirs_ref, ours_ref)):
        slots = dot(select_ref[part], high) + dot(select_ref[part], low)
        out_ref[...] = slots + earlier[part][...] if earlier else slots


def add_segment(picks, select, table, blocks, earlier=()):
    entries, (_, slots, _) = picks.shape[0] // 2, select.shape
    bins = table[0].shape[0] // 2
    operands = [picks, select, *table, *blocks, *earlier]
    in_vmem = pl.BlockSpec(memory_space=pltpu.VMEM)
    return pl.pallas_call(
        segment_kernel,
        out_shape=[jax.ShapeDtypeStruct((slots, LAGS), jnp.float32)] * 2,
        in_specs=[in_vmem] * len(operands),
        out_specs=[in_vmem] * 2,
        scratch_shapes=[pltpu.VMEM((entries, 2 * bins), jnp.bfloat16)] * 2,
        compiler_params=pltpu.CompilerParams(vmem_limit_bytes=24 * 1024 * 1024),
        cost_estimate=pl.CostEstimate(
            flops=4 * entries * (bins * (3 * LAGS + 2 * picks.shape[1]) + 2 * slots * LAGS),
            bytes_accessed=8 * bins * (LAGS + picks.shape[1]),
            transcendentals=0,
        ),
        name="add_segment",
    )(*operands)


def local_grid(spectra, pair_list, pair_stations, owner_code):
    own = spectra[0]
    stations, width = own.shape
    bins = width // 2
    catalogue = pair_stations.shape[1]
    capacity = 2 * catalogue // (ROWS * CORES)
    row, core = lax.axis_index("tm") // CORES, lax.axis_index("tm") % CORES
    layer, column = lax.axis_index("sta") // COLUMNS, lax.axis_index("sta") % COLUMNS
    after = lambda value, *others: lax.optimization_barrier((value, *others))[0]

    def around(value):
        return send(value, OTHER_COLUMN), send(value, OTHER_ROW)

    def diagonal(side, ahead):
        return send(jnp.where(core == 0, side, ahead), DIAGONAL)

    inner = (layer == 1) | (layer == 2)
    side, ahead = around(own)
    near, swapped = send(own, PAIR_SWAP), send(own, INNER_SWAP)
    corner = diagonal(side, ahead)
    third = jnp.where(inner, swapped, send(swapped, OUTWARD))
    two = jnp.concatenate([near, third], axis=0)
    two_side, two_ahead = around(two)
    swapped = send(near, INNER_SWAP)
    fourth = jnp.where(inner, swapped, send(swapped, OUTWARD))
    listed_here = pair_list[0, 0]
    listed_there = send(after(listed_here, third), OTHER_ROW)

    listed = jnp.stack([listed_here, listed_there])
    hit = listed[:, :, None] == jnp.arange(catalogue, dtype=jnp.int32)
    look_up = lambda values: jnp.sum(jnp.where(hit, values, 0), axis=-1)
    pair = jnp.concatenate([look_up(pair_stations[0]), look_up(pair_stations[1])], axis=1)
    holder, place = pair // stations, pair % stations
    apart = layer ^ (holder // COLUMNS)
    turns = jnp.where((apart > 1) & inner, 5 - apart, apart)
    beside = (holder % COLUMNS) ^ column
    position = (beside * LAYERS + turns) * stations + place
    spots = jnp.arange(COLUMNS * LAYERS * stations, dtype=jnp.int32)
    picks = (position[:, :, None] == spots).astype(jnp.bfloat16)

    fourth_side, fourth_ahead = around(after(fourth, picks))
    two_corner = diagonal(two_side, two_ahead)
    fourth_corner = diagonal(fourth_side, fourth_ahead)
    here = (own, two, fourth, side, two_side, fourth_side)
    there = (ahead, two_ahead, fourth_ahead)
    there += (corner, two_corner, fourth_corner)

    codes = look_up(owner_code)
    owner = row * CORES + jnp.stack([1 - core, core])
    slots = owner[:, None] * capacity + jnp.arange(capacity, dtype=jnp.int32)
    select = (slots[:, :, None] == codes[:, None, None, :]).astype(jnp.bfloat16)

    table = split_table(bins)
    sums = add_segment(picks[0], select[0], table, here)
    theirs, ours = add_segment(picks[1], select[1], table, there, sums)
    return ours + send(theirs, OTHER_CORE)


def solution(mesh):
    sizes = (mesh.shape["tm"], mesh.shape["sta"])
    fits = sizes == (ROWS * CORES, LAYERS * COLUMNS)
    return jax.shard_map(
        local_grid if fits else local_any_size,
        mesh=mesh,
        in_specs=(P("tm", "sta", None), P("tm", "sta", None), P(None, "sta"), P("sta")),
        out_specs=P(("tm", "sta"), None),
        check_vma=False,
    )
```

```python
import functools

import jax
import jax.numpy as jnp
import numpy as np
from jax import lax
from jax.experimental import pallas as pl
from jax.experimental.pallas import tpu as pltpu
from jax.sharding import PartitionSpec as P

LAGS = 1024
AXES = ("tm", "sta")
ROWS, CORES, LAYERS, COLUMNS = 2, 2, 4, 2
BLOCK = 256


def lag_table(bins, lags):
    bin_index = jnp.arange(bins, dtype=jnp.int32)[:, None]
    lag_index = jnp.arange(lags, dtype=jnp.int32)[None, :] - lags // 2
    phase = (bin_index * lag_index % (2 * bins)).astype(jnp.float32) * (jnp.pi / bins)
    scale = 1.0 / bins**0.5
    return jnp.concatenate([jnp.cos(phase) * scale, -jnp.sin(phase) * scale], axis=0)


def cross_spectra(first, second, bins):
    first = first.astype(jnp.float32)
    second = second.astype(jnp.float32)
    real_a, imag_a = (first[..., :bins], first[..., bins:])
    real_b, imag_b = (second[..., :bins], second[..., bins:])
    real_c = real_a * real_b + imag_a * imag_b
    imag_c = real_a * imag_b - imag_a * real_b
    return jnp.concatenate([real_c, imag_c], axis=-1)


def local_any_size(spectra, pair_list, pair_stations, owner_code):
    local_spectra = spectra[0]
    width = local_spectra.shape[1]
    bins = width // 2
    catalogue = pair_stations.shape[1]
    groups = lax.axis_size("tm")
    capacity = 2 * catalogue // groups
    listed = pair_list[0, 0]
    first_station = pair_stations[0][listed]
    second_station = pair_stations[1][listed]
    codes = owner_code[listed]
    table = lag_table(bins, LAGS)
    all_spectra = lax.all_gather(local_spectra, "sta", axis=0, tiled=True)
    first = all_spectra[first_station]
    second = all_spectra[second_station]
    cross = cross_spectra(first, second, bins)
    partial_lags = jnp.dot(
        cross, table, precision=lax.Precision.HIGHEST, preferred_element_type=jnp.float32
    )
    slots = jnp.arange(capacity * lax.axis_size("tm"), dtype=jnp.int32)
    select = (slots[:, None] == codes[None, :]).astype(jnp.float32)
    return lax.psum_scatter(
        jnp.dot(
            select,
            partial_lags,
            precision=lax.Precision.HIGHEST,
            preferred_element_type=jnp.float32,
        ),
        "tm",
        scatter_dimension=0,
        tiled=True,
    )


def moves(target):
    def place(row, core, layer, column):
        return (row * CORES + core) * LAYERS * COLUMNS + layer * COLUMNS + column

    return [
        (place(row, core, layer, column), place(*to))
        for row in range(ROWS)
        for core in range(CORES)
        for layer in range(LAYERS)
        for column in range(COLUMNS)
        if (to := target(row, core, layer, column)) is not None
    ]


OTHER_ROW = moves(lambda r, c, z, x: (1 - r, c, z, x))
OTHER_CORE = moves(lambda r, c, z, x: (r, 1 - c, z, x))
OTHER_COLUMN = moves(lambda r, c, z, x: (r, c, z, 1 - x))
DIAGONAL = moves(lambda r, c, z, x: (1 - r, c, z, x) if c == 0 else (r, c, z, 1 - x))
PAIR_SWAP = moves(lambda r, c, z, x: (r, c, z ^ 1, x))
INNER_SWAP = moves(lambda r, c, z, x: (r, c, 3 - z, x) if z in (1, 2) else (r, 1 - c, z, x))
OUTWARD = PAIR_SWAP


def send(value, pairs):
    return lax.ppermute(value, AXES, pairs)


def split_table(bins):
    index = np.arange(bins)[:, None] * np.arange(LAGS // 2)[None, :] % (2 * bins)
    angle = index * (np.pi / bins)
    rows = np.concatenate([np.cos(angle), np.sin(angle)]) / np.sqrt(bins)
    rows = rows.astype(np.float32)
    high = rows.astype(jnp.bfloat16)
    low = (rows - high.astype(np.float32)).astype(jnp.bfloat16)
    return jnp.asarray(high), jnp.asarray(low)


def first_lag(bins):
    index = np.arange(bins) * (LAGS // 2) % (2 * bins)
    angle = index * (np.pi / bins)
    return jnp.asarray(np.stack([np.cos(angle), np.sin(angle)]) / np.sqrt(bins), jnp.float32)


def backwards():
    half = LAGS // 2
    return jnp.asarray(np.arange(half)[:, None] == -np.arange(half)[None, :] % half, jnp.bfloat16)


def two_parts(value):
    high = value.astype(jnp.bfloat16)
    return high, (value - high.astype(jnp.float32)).astype(jnp.bfloat16)


def segment_kernel(picks_ref, select_ref, table_high, table_low, first_ref, back_ref, *refs):
    blocks, refs = refs[:6], refs[6:]
    earlier, (theirs_ref, ours_ref, high_cross, low_cross) = refs[:-4], refs[-4:]
    entries = picks_ref.shape[0] // 2
    bins = table_high.shape[0] // 2
    dot = functools.partial(jnp.dot, preferred_element_type=jnp.float32)

    half = LAGS // 2
    first = jnp.zeros((entries, 1), jnp.float32)
    for at in range(0, bins, BLOCK):
        real, imag = slice(at, at + BLOCK), slice(bins + at, bins + at + BLOCK)
        stations = jnp.concatenate(
            [jnp.concatenate([ref[:, real], ref[:, imag]], axis=1) for ref in blocks], axis=0
        )
        both = dot(picks_ref[...], stations)
        real_a, imag_a = both[:entries, :BLOCK], both[:entries, BLOCK:]
        real_b, imag_b = both[entries:, :BLOCK], both[entries:, BLOCK:]
        real_c = real_a * real_b + imag_a * imag_b
        imag_c = real_a * imag_b - imag_a * real_b
        high_cross[:, real], low_cross[:, real] = two_parts(real_c)
        high_cross[:, imag], low_cross[:, imag] = two_parts(imag_c)
        terms = real_c * first_ref[0:1, real] + imag_c * first_ref[1:2, real]
        first += jnp.sum(terms, axis=1, keepdims=True)

    even, odd = (
        dot(high_cross[:, part], table_high[part, :])
        + dot(low_cross[:, part], table_high[part, :])
        + dot(high_cross[:, part], table_low[part, :])
        for part in (slice(0, bins), slice(bins, 2 * bins))
    )
    column = lax.broadcasted_iota(jnp.int32, even.shape, 1)
    before = jnp.where(column == 0, first, even + odd)
    high, low = (
        jnp.concatenate([dot(early, back_ref[...]).astype(jnp.bfloat16), late], axis=1)
        for early, late in zip(two_parts(before), two_parts(even - odd))
    )
    for part, out_ref in enumerate((theirs_ref, ours_ref)):
        slots = dot(select_ref[part], high) + dot(select_ref[part], low)
        out_ref[...] = slots + earlier[part][...] if earlier else slots


def add_segment(picks, select, table, blocks, earlier=()):
    entries, (_, slots, _) = picks.shape[0] // 2, select.shape
    bins = table[0].shape[0] // 2
    operands = [picks, select, *table, first_lag(bins), backwards(), *blocks, *earlier]
    in_vmem = pl.BlockSpec(memory_space=pltpu.VMEM)
    return pl.pallas_call(
        segment_kernel,
        out_shape=[jax.ShapeDtypeStruct((slots, LAGS), jnp.float32)] * 2,
        in_specs=[in_vmem] * len(operands),
        out_specs=[in_vmem] * 2,
        scratch_shapes=[pltpu.VMEM((entries, 2 * bins), jnp.bfloat16)] * 2,
        compiler_params=pltpu.CompilerParams(vmem_limit_bytes=24 * 1024 * 1024),
        cost_estimate=pl.CostEstimate(
            flops=2 * entries * LAGS * (3 * bins + LAGS // 2 + 4 * slots)
            + 8 * entries * bins * picks.shape[1],
            bytes_accessed=8 * bins * (LAGS + picks.shape[1]),
            transcendentals=0,
        ),
        name="add_segment",
    )(*operands)


def local_grid(spectra, pair_list, pair_stations, owner_code):
    own = spectra[0]
    stations, width = own.shape
    bins = width // 2
    catalogue = pair_stations.shape[1]
    capacity = 2 * catalogue // (ROWS * CORES)
    row, core = lax.axis_index("tm") // CORES, lax.axis_index("tm") % CORES
    layer, column = lax.axis_index("sta") // COLUMNS, lax.axis_index("sta") % COLUMNS
    after = lambda value, *others: lax.optimization_barrier((value, *others))[0]

    def around(value):
        return send(value, OTHER_COLUMN), send(value, OTHER_ROW)

    def diagonal(side, ahead):
        return send(jnp.where(core == 0, side, ahead), DIAGONAL)

    inner = (layer == 1) | (layer == 2)
    side, ahead = around(own)
    near, swapped = send(own, PAIR_SWAP), send(own, INNER_SWAP)
    corner = diagonal(side, ahead)
    third = jnp.where(inner, swapped, send(swapped, OUTWARD))
    two = jnp.concatenate([near, third], axis=0)
    two_side, two_ahead = around(two)
    swapped = send(near, INNER_SWAP)
    fourth = jnp.where(inner, swapped, send(swapped, OUTWARD))
    listed_here = pair_list[0, 0]
    listed_there = send(after(listed_here, third), OTHER_ROW)

    listed = jnp.stack([listed_here, listed_there])
    hit = listed[:, :, None] == jnp.arange(catalogue, dtype=jnp.int32)
    look_up = lambda values: jnp.sum(jnp.where(hit, values, 0), axis=-1)
    pair = jnp.concatenate([look_up(pair_stations[0]), look_up(pair_stations[1])], axis=1)
    holder, place = pair // stations, pair % stations
    apart = layer ^ (holder // COLUMNS)
    turns = jnp.where((apart > 1) & inner, 5 - apart, apart)
    beside = (holder % COLUMNS) ^ column
    position = (beside * LAYERS + turns) * stations + place
    spots = jnp.arange(COLUMNS * LAYERS * stations, dtype=jnp.int32)
    picks = (position[:, :, None] == spots).astype(jnp.bfloat16)

    fourth_side, fourth_ahead = around(after(fourth, picks))
    two_corner = diagonal(two_side, two_ahead)
    fourth_corner = diagonal(fourth_side, fourth_ahead)
    here = (own, two, fourth, side, two_side, fourth_side)
    there = (ahead, two_ahead, fourth_ahead)
    there += (corner, two_corner, fourth_corner)

    codes = look_up(owner_code)
    owner = row * CORES + jnp.stack([1 - core, core])
    slots = owner[:, None] * capacity + jnp.arange(capacity, dtype=jnp.int32)
    select = (slots[:, :, None] == codes[:, None, None, :]).astype(jnp.bfloat16)

    table = split_table(bins)
    sums = add_segment(picks[0], select[0], table, here)
    theirs, ours = add_segment(picks[1], select[1], table, there, sums)
    return ours + send(theirs, OTHER_CORE)


def solution(mesh):
    sizes = (mesh.shape["tm"], mesh.shape["sta"])
    fits = sizes == (ROWS * CORES, LAYERS * COLUMNS)
    return jax.shard_map(
        local_grid if fits else local_any_size,
        mesh=mesh,
        in_specs=(P("tm", "sta", None), P("tm", "sta", None), P(None, "sta"), P("sta")),
        out_specs=P(("tm", "sta"), None),
        check_vma=False,
    )
```

```python
import functools

import jax
import jax.numpy as jnp
import numpy as np
from jax import lax
from jax.experimental import pallas as pl
from jax.experimental.pallas import tpu as pltpu
from jax.sharding import PartitionSpec as P

LAGS = 1024
AXES = ("tm", "sta")
ROWS, CORES, LAYERS, COLUMNS = 2, 2, 4, 2
BLOCK = 256


def lag_table(bins, lags):
    bin_index = jnp.arange(bins, dtype=jnp.int32)[:, None]
    lag_index = jnp.arange(lags, dtype=jnp.int32)[None, :] - lags // 2
    phase = (bin_index * lag_index % (2 * bins)).astype(jnp.float32) * (jnp.pi / bins)
    scale = 1.0 / bins**0.5
    return jnp.concatenate([jnp.cos(phase) * scale, -jnp.sin(phase) * scale], axis=0)


def cross_spectra(first, second, bins):
    first = first.astype(jnp.float32)
    second = second.astype(jnp.float32)
    real_a, imag_a = (first[..., :bins], first[..., bins:])
    real_b, imag_b = (second[..., :bins], second[..., bins:])
    real_c = real_a * real_b + imag_a * imag_b
    imag_c = real_a * imag_b - imag_a * real_b
    return jnp.concatenate([real_c, imag_c], axis=-1)


def local_any_size(spectra, pair_list, pair_stations, owner_code):
    local_spectra = spectra[0]
    width = local_spectra.shape[1]
    bins = width // 2
    catalogue = pair_stations.shape[1]
    groups = lax.axis_size("tm")
    capacity = 2 * catalogue // groups
    listed = pair_list[0, 0]
    first_station = pair_stations[0][listed]
    second_station = pair_stations[1][listed]
    codes = owner_code[listed]
    table = lag_table(bins, LAGS)
    all_spectra = lax.all_gather(local_spectra, "sta", axis=0, tiled=True)
    first = all_spectra[first_station]
    second = all_spectra[second_station]
    cross = cross_spectra(first, second, bins)
    partial_lags = jnp.dot(
        cross, table, precision=lax.Precision.HIGHEST, preferred_element_type=jnp.float32
    )
    slots = jnp.arange(capacity * lax.axis_size("tm"), dtype=jnp.int32)
    select = (slots[:, None] == codes[None, :]).astype(jnp.float32)
    return lax.psum_scatter(
        jnp.dot(
            select,
            partial_lags,
            precision=lax.Precision.HIGHEST,
            preferred_element_type=jnp.float32,
        ),
        "tm",
        scatter_dimension=0,
        tiled=True,
    )


def moves(target):
    def place(row, core, layer, column):
        return (row * CORES + core) * LAYERS * COLUMNS + layer * COLUMNS + column

    return [
        (place(row, core, layer, column), place(*to))
        for row in range(ROWS)
        for core in range(CORES)
        for layer in range(LAYERS)
        for column in range(COLUMNS)
        if (to := target(row, core, layer, column)) is not None
    ]


OTHER_ROW = moves(lambda r, c, z, x: (1 - r, c, z, x))
OTHER_CORE = moves(lambda r, c, z, x: (r, 1 - c, z, x))
OTHER_COLUMN = moves(lambda r, c, z, x: (r, c, z, 1 - x))
DIAGONAL = moves(lambda r, c, z, x: (1 - r, c, z, x) if c == 0 else (r, c, z, 1 - x))
PAIR_SWAP = moves(lambda r, c, z, x: (r, c, z ^ 1, x))
INNER_SWAP = moves(lambda r, c, z, x: (r, c, 3 - z, x) if z in (1, 2) else (r, 1 - c, z, x))
OUTWARD = PAIR_SWAP


def send(value, pairs):
    return lax.ppermute(value, AXES, pairs)


def split_table(bins):
    index = np.arange(bins)[:, None] * np.arange(LAGS // 2)[None, :] % (2 * bins)
    angle = index * (np.pi / bins)
    rows = np.concatenate([np.cos(angle), np.sin(angle)]) / np.sqrt(bins)
    rows = rows.astype(np.float32)
    high = rows.astype(jnp.bfloat16)
    low = (rows - high.astype(np.float32)).astype(jnp.bfloat16)
    return jnp.asarray(high), jnp.asarray(low)


def first_lag(bins):
    index = np.arange(bins) * (LAGS // 2) % (2 * bins)
    angle = index * (np.pi / bins)
    return jnp.asarray(np.stack([np.cos(angle), np.sin(angle)]) / np.sqrt(bins), jnp.float32)


def backwards():
    half = LAGS // 2
    return jnp.asarray(np.arange(half)[:, None] == -np.arange(half)[None, :] % half, jnp.bfloat16)


def two_parts(value):
    high = value.astype(jnp.bfloat16)
    return high, (value - high.astype(jnp.float32)).astype(jnp.bfloat16)


def segment_kernel(count, rows, picks_ref, select_ref, table_high, table_low, first_ref, back_ref, *refs):
    blocks, refs = refs[:count], refs[count:]
    earlier, (theirs_ref, high_ref, low_ref, high_cross, low_cross) = refs[:-5], refs[-5:]
    entries = picks_ref.shape[0] // 2
    bins = table_high.shape[0] // 2
    dot = functools.partial(jnp.dot, preferred_element_type=jnp.float32)

    half = LAGS // 2
    first = jnp.zeros((entries, 1), jnp.float32)
    for at in range(0, bins, BLOCK):
        real, imag = slice(at, at + BLOCK), slice(bins + at, bins + at + BLOCK)
        stations = jnp.concatenate(
            [
                jnp.concatenate([ref[:many, real], ref[:many, imag]], axis=1)
                for ref, many in zip(blocks, rows)
            ],
            axis=0,
        )
        both = dot(picks_ref[...], stations)
        real_a, imag_a = both[:entries, :BLOCK], both[:entries, BLOCK:]
        real_b, imag_b = both[entries:, :BLOCK], both[entries:, BLOCK:]
        real_c = real_a * real_b + imag_a * imag_b
        imag_c = real_a * imag_b - imag_a * real_b
        high_cross[:, real], low_cross[:, real] = two_parts(real_c)
        high_cross[:, imag], low_cross[:, imag] = two_parts(imag_c)
        terms = real_c * first_ref[0:1, real] + imag_c * first_ref[1:2, real]
        first += jnp.sum(terms, axis=1, keepdims=True)

    even, odd = (
        dot(high_cross[:, part], table_high[part, :])
        + dot(low_cross[:, part], table_high[part, :])
        + dot(high_cross[:, part], table_low[part, :])
        for part in (slice(0, bins), slice(bins, 2 * bins))
    )
    column = lax.broadcasted_iota(jnp.int32, even.shape, 1)
    before = jnp.where(column == 0, first, even + odd)
    high, low = (
        jnp.concatenate([dot(early, back_ref[...]).astype(jnp.bfloat16), late], axis=1)
        for early, late in zip(two_parts(before), two_parts(even - odd))
    )
    high_ref[...], low_ref[...] = high, low
    slots = dot(select_ref[...], high) + dot(select_ref[...], low)
    theirs_ref[...] = slots + earlier[0][...] if earlier else slots


def slots_kernel(select_ref, *refs):
    parts, out_ref = refs[:-1], refs[-1]
    out_ref[...] = sum(
        jnp.dot(select_ref[at // 2], part[...], preferred_element_type=jnp.float32)
        for at, part in enumerate(parts)
    )


def add_segment(picks, select, table, blocks, stations, earlier=()):
    entries, slots = picks.shape[0] // 2, select.shape[0]
    rows = [block.shape[0] // stations * stations for block in blocks]
    bins = table[0].shape[0] // 2
    operands = [picks, select, *table, first_lag(bins), backwards(), *blocks, *earlier]
    in_vmem = pl.BlockSpec(memory_space=pltpu.VMEM)
    return pl.pallas_call(
        functools.partial(segment_kernel, len(blocks), rows),
        out_shape=[jax.ShapeDtypeStruct((slots, LAGS), jnp.float32)]
        + [jax.ShapeDtypeStruct((entries, LAGS), jnp.bfloat16)] * 2,
        in_specs=[in_vmem] * len(operands),
        out_specs=[in_vmem] * 3,
        scratch_shapes=[pltpu.VMEM((entries, 2 * bins), jnp.bfloat16)] * 2,
        compiler_params=pltpu.CompilerParams(vmem_limit_bytes=24 * 1024 * 1024),
        cost_estimate=pl.CostEstimate(
            flops=2 * entries * LAGS * (3 * bins + LAGS // 2 + 2 * slots)
            + 8 * entries * bins * picks.shape[1],
            bytes_accessed=8 * bins * (LAGS + picks.shape[1]),
            transcendentals=0,
        ),
        name="add_segment",
    )(*operands)


def add_slots(select, parts):
    in_vmem = pl.BlockSpec(memory_space=pltpu.VMEM)
    return pl.pallas_call(
        slots_kernel,
        out_shape=jax.ShapeDtypeStruct((select.shape[1], LAGS), jnp.float32),
        in_specs=[in_vmem] * (1 + len(parts)),
        out_specs=in_vmem,
        compiler_params=pltpu.CompilerParams(vmem_limit_bytes=16 * 1024 * 1024),
        cost_estimate=pl.CostEstimate(
            flops=2 * len(parts) * parts[0].size * select.shape[1],
            bytes_accessed=4 * len(parts) * parts[0].size,
            transcendentals=0,
        ),
        name="add_slots",
    )(select, *parts)


def local_grid(spectra, pair_list, pair_stations, owner_code):
    own = spectra[0]
    stations, width = own.shape
    bins = width // 2
    catalogue = pair_stations.shape[1]
    capacity = 2 * catalogue // (ROWS * CORES)
    row, core = lax.axis_index("tm") // CORES, lax.axis_index("tm") % CORES
    layer, column = lax.axis_index("sta") // COLUMNS, lax.axis_index("sta") % COLUMNS
    after = lambda value, *others: lax.optimization_barrier((value, *others))[0]

    def around(value):
        return send(value, OTHER_COLUMN), send(value, OTHER_ROW)

    def diagonal(side, ahead):
        return send(jnp.where(core == 0, side, ahead), DIAGONAL)

    listed_here = pair_list[0, 0]
    inner = (layer == 1) | (layer == 2)
    side, ahead = around(own)
    near, m1 = send(own, PAIR_SWAP), send(own, INNER_SWAP)
    l1 = send(m1, OUTWARD)
    third = jnp.where(inner, m1, l1)
    m2 = send(near, INNER_SWAP)
    corner = send(jnp.where(core == 0, side, ahead), DIAGONAL)
    two = jnp.concatenate([near, third], axis=0)
    two_side, two_ahead = around(two)
    l2 = send(m2, OUTWARD)
    fourth = jnp.where(inner, m2, l2)
    listed_there = send(after(listed_here, third), OTHER_ROW)

    listed = jnp.stack([listed_here, listed_there])
    hit = listed[:, :, None] == jnp.arange(catalogue, dtype=jnp.int32)
    look_up = lambda values: jnp.sum(jnp.where(hit, values, 0), axis=-1)
    pair = jnp.concatenate([look_up(pair_stations[0]), look_up(pair_stations[1])], axis=1)
    holder, place = pair // stations, pair % stations
    apart = layer ^ (holder // COLUMNS)
    turns = jnp.where((apart > 1) & inner, 5 - apart, apart)
    beside = (holder % COLUMNS) ^ column
    position = (beside * LAYERS + turns) * stations + place
    spots = jnp.arange(COLUMNS * LAYERS * stations, dtype=jnp.int32)
    picks = (position[:, :, None] == spots).astype(jnp.bfloat16)

    fourth_side, fourth_ahead = around(after(fourth, picks))
    inward = send(after(corner, third), INNER_SWAP)
    outward = send(after(jnp.concatenate([corner, inward], axis=0), fourth), OUTWARD)
    near_corner = outward[:stations]
    third_corner = jnp.where(inner, inward, outward[stations:])
    fourth_corner = send(jnp.where(core == 0, fourth_side, fourth_ahead), DIAGONAL)
    here = (own, two, fourth, side, two_side, fourth_side)
    there = (ahead, two_ahead, fourth_ahead, corner, near_corner, third_corner, fourth_corner)

    codes = look_up(owner_code)
    owner = row * CORES + jnp.stack([1 - core, core])
    slots = owner[:, None] * capacity + jnp.arange(capacity, dtype=jnp.int32)
    select = (slots[:, :, None] == codes[:, None, None, :]).astype(jnp.bfloat16)

    table = split_table(bins)
    theirs, *first_parts = add_segment(picks[0], select[0, 0], table, here, stations)
    theirs, *parts = add_segment(picks[1], select[1, 0], table, there, stations, [theirs])
    ours = add_slots(select[:, 1], first_parts + parts)
    return ours + send(theirs, OTHER_CORE)


def solution(mesh):
    sizes = (mesh.shape["tm"], mesh.shape["sta"])
    fits = sizes == (ROWS * CORES, LAYERS * COLUMNS)
    return jax.shard_map(
        local_grid if fits else local_any_size,
        mesh=mesh,
        in_specs=(P("tm", "sta", None), P("tm", "sta", None), P(None, "sta"), P("sta")),
        out_specs=P(("tm", "sta"), None),
        check_vma=False,
    )
```

```python
import functools

import jax
import jax.numpy as jnp
import numpy as np
from jax import lax
from jax.experimental import pallas as pl
from jax.experimental.pallas import tpu as pltpu
from jax.sharding import PartitionSpec as P

LAGS = 1024
AXES = ("tm", "sta")
ROWS, CORES, LAYERS, COLUMNS = 2, 2, 4, 2
BLOCK = 256


def lag_table(bins, lags):
    bin_index = jnp.arange(bins, dtype=jnp.int32)[:, None]
    lag_index = jnp.arange(lags, dtype=jnp.int32)[None, :] - lags // 2
    phase = (bin_index * lag_index % (2 * bins)).astype(jnp.float32) * (jnp.pi / bins)
    scale = 1.0 / bins**0.5
    return jnp.concatenate([jnp.cos(phase) * scale, -jnp.sin(phase) * scale], axis=0)


def cross_spectra(first, second, bins):
    first = first.astype(jnp.float32)
    second = second.astype(jnp.float32)
    real_a, imag_a = (first[..., :bins], first[..., bins:])
    real_b, imag_b = (second[..., :bins], second[..., bins:])
    real_c = real_a * real_b + imag_a * imag_b
    imag_c = real_a * imag_b - imag_a * real_b
    return jnp.concatenate([real_c, imag_c], axis=-1)


def local_any_size(spectra, pair_list, pair_stations, owner_code):
    local_spectra = spectra[0]
    width = local_spectra.shape[1]
    bins = width // 2
    catalogue = pair_stations.shape[1]
    groups = lax.axis_size("tm")
    capacity = 2 * catalogue // groups
    listed = pair_list[0, 0]
    first_station = pair_stations[0][listed]
    second_station = pair_stations[1][listed]
    codes = owner_code[listed]
    table = lag_table(bins, LAGS)
    all_spectra = lax.all_gather(local_spectra, "sta", axis=0, tiled=True)
    first = all_spectra[first_station]
    second = all_spectra[second_station]
    cross = cross_spectra(first, second, bins)
    partial_lags = jnp.dot(
        cross, table, precision=lax.Precision.HIGHEST, preferred_element_type=jnp.float32
    )
    slots = jnp.arange(capacity * lax.axis_size("tm"), dtype=jnp.int32)
    select = (slots[:, None] == codes[None, :]).astype(jnp.float32)
    return lax.psum_scatter(
        jnp.dot(
            select,
            partial_lags,
            precision=lax.Precision.HIGHEST,
            preferred_element_type=jnp.float32,
        ),
        "tm",
        scatter_dimension=0,
        tiled=True,
    )


def moves(target):
    def place(row, core, layer, column):
        return (row * CORES + core) * LAYERS * COLUMNS + layer * COLUMNS + column

    return [
        (place(row, core, layer, column), place(*to))
        for row in range(ROWS)
        for core in range(CORES)
        for layer in range(LAYERS)
        for column in range(COLUMNS)
        if (to := target(row, core, layer, column)) is not None
    ]


OTHER_ROW = moves(lambda r, c, z, x: (1 - r, c, z, x))
OTHER_CORE = moves(lambda r, c, z, x: (r, 1 - c, z, x))
OTHER_COLUMN = moves(lambda r, c, z, x: (r, c, z, 1 - x))
DIAGONAL = moves(lambda r, c, z, x: (1 - r, c, z, x) if c == 0 else (r, c, z, 1 - x))
PAIR_SWAP = moves(lambda r, c, z, x: (r, c, z ^ 1, x))
INNER_SWAP = moves(lambda r, c, z, x: (r, c, 3 - z, x) if z in (1, 2) else (r, 1 - c, z, x))
OUTWARD = PAIR_SWAP


def send(value, pairs):
    return lax.ppermute(value, AXES, pairs)


def split_table(bins):
    index = np.arange(bins)[:, None] * np.arange(LAGS // 2)[None, :] % (2 * bins)
    angle = index * (np.pi / bins)
    rows = np.concatenate([np.cos(angle), np.sin(angle)]) / np.sqrt(bins)
    rows = rows.astype(np.float32)
    high = rows.astype(jnp.bfloat16)
    low = (rows - high.astype(np.float32)).astype(jnp.bfloat16)
    return jnp.asarray(high), jnp.asarray(low)


def first_lag(bins):
    index = np.arange(bins) * (LAGS // 2) % (2 * bins)
    angle = index * (np.pi / bins)
    return jnp.asarray(np.stack([np.cos(angle), np.sin(angle)]) / np.sqrt(bins), jnp.float32)


def backwards():
    half = LAGS // 2
    return jnp.asarray(np.arange(half)[:, None] == -np.arange(half)[None, :] % half, jnp.bfloat16)


def two_parts(value):
    high = value.astype(jnp.bfloat16)
    return high, (value - high.astype(jnp.float32)).astype(jnp.bfloat16)


def segment_kernel(count, rows, picks_ref, select_ref, table_high, table_low, first_ref, back_ref, *refs):
    blocks, refs = refs[:count], refs[count:]
    earlier, (theirs_ref, high_ref, low_ref, high_cross, low_cross) = refs[:-5], refs[-5:]
    entries = picks_ref.shape[0] // 2
    bins = table_high.shape[0] // 2
    dot = functools.partial(jnp.dot, preferred_element_type=jnp.float32)

    first = jnp.zeros((entries, BLOCK), jnp.float32)
    for at in range(0, bins, BLOCK):
        real, imag = slice(at, at + BLOCK), slice(bins + at, bins + at + BLOCK)
        stations = jnp.concatenate(
            [
                jnp.concatenate([ref[:many, real], ref[:many, imag]], axis=1)
                for ref, many in zip(blocks, rows)
            ],
            axis=0,
        )
        both = dot(picks_ref[...], stations)
        real_a, imag_a = both[:entries, :BLOCK], both[:entries, BLOCK:]
        real_b, imag_b = both[entries:, :BLOCK], both[entries:, BLOCK:]
        real_c = real_a * real_b + imag_a * imag_b
        imag_c = real_a * imag_b - imag_a * real_b
        high_cross[:, real], low_cross[:, real] = two_parts(real_c)
        high_cross[:, imag], low_cross[:, imag] = two_parts(imag_c)
        first += real_c * first_ref[0:1, real] + imag_c * first_ref[1:2, real]

    even, odd = (
        dot(high_cross[:, part], table_high[part, :])
        + dot(low_cross[:, part], table_high[part, :])
        + dot(high_cross[:, part], table_low[part, :])
        for part in (slice(0, bins), slice(bins, 2 * bins))
    )
    column = lax.broadcasted_iota(jnp.int32, even.shape, 1)
    before = jnp.where(column == 0, jnp.sum(first, axis=1, keepdims=True), even + odd)
    high, low = (
        jnp.concatenate([dot(early, back_ref[...]).astype(jnp.bfloat16), late], axis=1)
        for early, late in zip(two_parts(before), two_parts(even - odd))
    )
    high_ref[...], low_ref[...] = high, low
    slots = dot(select_ref[...], high) + dot(select_ref[...], low)
    theirs_ref[...] = slots + earlier[0][...] if earlier else slots


def slots_kernel(select_ref, *refs):
    parts, out_ref = refs[:-1], refs[-1]
    out_ref[...] = sum(
        jnp.dot(select_ref[at // 2], part[...], preferred_element_type=jnp.float32)
        for at, part in enumerate(parts)
    )


def add_segment(picks, select, table, blocks, stations, earlier=()):
    entries, slots = picks.shape[0] // 2, select.shape[0]
    rows = [block.shape[0] // stations * stations for block in blocks]
    bins = table[0].shape[0] // 2
    operands = [picks, select, *table, first_lag(bins), backwards(), *blocks, *earlier]
    in_vmem = pl.BlockSpec(memory_space=pltpu.VMEM)
    return pl.pallas_call(
        functools.partial(segment_kernel, len(blocks), rows),
        out_shape=[jax.ShapeDtypeStruct((slots, LAGS), jnp.float32)]
        + [jax.ShapeDtypeStruct((entries, LAGS), jnp.bfloat16)] * 2,
        in_specs=[in_vmem] * len(operands),
        out_specs=[in_vmem] * 3,
        scratch_shapes=[pltpu.VMEM((entries, 2 * bins), jnp.bfloat16)] * 2,
        compiler_params=pltpu.CompilerParams(vmem_limit_bytes=24 * 1024 * 1024),
        cost_estimate=pl.CostEstimate(
            flops=2 * entries * LAGS * (3 * bins + LAGS // 2 + 2 * slots)
            + 8 * entries * bins * picks.shape[1],
            bytes_accessed=8 * bins * (LAGS + picks.shape[1]),
            transcendentals=0,
        ),
        name="add_segment",
    )(*operands)


def add_slots(select, parts):
    in_vmem = pl.BlockSpec(memory_space=pltpu.VMEM)
    return pl.pallas_call(
        slots_kernel,
        out_shape=jax.ShapeDtypeStruct((select.shape[1], LAGS), jnp.float32),
        in_specs=[in_vmem] * (1 + len(parts)),
        out_specs=in_vmem,
        compiler_params=pltpu.CompilerParams(vmem_limit_bytes=16 * 1024 * 1024),
        cost_estimate=pl.CostEstimate(
            flops=2 * len(parts) * parts[0].size * select.shape[1],
            bytes_accessed=4 * len(parts) * parts[0].size,
            transcendentals=0,
        ),
        name="add_slots",
    )(select, *parts)


def local_grid(spectra, pair_list, pair_stations, owner_code):
    own = spectra[0]
    stations, width = own.shape
    bins = width // 2
    catalogue = pair_stations.shape[1]
    capacity = 2 * catalogue // (ROWS * CORES)
    row, core = lax.axis_index("tm") // CORES, lax.axis_index("tm") % CORES
    layer, column = lax.axis_index("sta") // COLUMNS, lax.axis_index("sta") % COLUMNS
    after = lambda value, *others: lax.optimization_barrier((value, *others))[0]

    def around(value):
        return send(value, OTHER_COLUMN), send(value, OTHER_ROW)

    def diagonal(side, ahead):
        return send(jnp.where(core == 0, side, ahead), DIAGONAL)

    listed_here = pair_list[0, 0]
    inner = (layer == 1) | (layer == 2)
    side, ahead = around(own)
    near, swapped = send(own, PAIR_SWAP), send(own, INNER_SWAP)
    third = jnp.where(inner, swapped, send(swapped, OUTWARD))
    swapped = send(near, INNER_SWAP)
    corner = diagonal(side, ahead)
    two = jnp.concatenate([near, third], axis=0)
    two_side, two_ahead = around(two)
    fourth = jnp.where(inner, swapped, send(swapped, OUTWARD))
    listed_there = send(after(listed_here, third), OTHER_ROW)

    listed = jnp.stack([listed_here, listed_there])
    hit = listed[:, :, None] == jnp.arange(catalogue, dtype=jnp.int32)
    look_up = lambda values: jnp.sum(jnp.where(hit, values, 0), axis=-1)
    pair = jnp.concatenate([look_up(pair_stations[0]), look_up(pair_stations[1])], axis=1)
    holder, place = pair // stations, pair % stations
    apart = layer ^ (holder // COLUMNS)
    turns = jnp.where((apart > 1) & inner, 5 - apart, apart)
    beside = (holder % COLUMNS) ^ column
    position = (beside * LAYERS + turns) * stations + place
    spots = jnp.arange(COLUMNS * LAYERS * stations, dtype=jnp.int32)
    picks = (position[:, :, None] == spots).astype(jnp.bfloat16)

    fourth_side, fourth_ahead = around(after(fourth, picks))
    inward = send(after(corner, third), INNER_SWAP)
    outward = send(after(jnp.concatenate([corner, inward], axis=0), fourth), OUTWARD)
    near_corner = outward[:stations]
    third_corner = jnp.where(inner, inward, outward[stations:])
    fourth_corner = diagonal(fourth_side, fourth_ahead)
    here = (own, two, fourth, side, two_side, fourth_side)
    there = (ahead, two_ahead, fourth_ahead, corner, near_corner, third_corner, fourth_corner)

    codes = look_up(owner_code)
    owner = row * CORES + jnp.stack([1 - core, core])
    slots = owner[:, None] * capacity + jnp.arange(capacity, dtype=jnp.int32)
    select = (slots[:, :, None] == codes[:, None, None, :]).astype(jnp.bfloat16)

    table = split_table(bins)
    theirs, *first_parts = add_segment(picks[0], select[0, 0], table, here, stations)
    theirs, *parts = add_segment(picks[1], select[1, 0], table, there, stations, [theirs])
    ours = add_slots(select[:, 1], first_parts + parts)
    return ours + send(theirs, OTHER_CORE)


def solution(mesh):
    sizes = (mesh.shape["tm"], mesh.shape["sta"])
    fits = sizes == (ROWS * CORES, LAYERS * COLUMNS)
    return jax.shard_map(
        local_grid if fits else local_any_size,
        mesh=mesh,
        in_specs=(P("tm", "sta", None), P("tm", "sta", None), P(None, "sta"), P("sta")),
        out_specs=P(("tm", "sta"), None),
        check_vma=False,
    )
```
